32 devices in a mesh: groups: 2 (over y), date: 4 (over z), pix: 2 (over x), chan: 2 (over core).
Axes of the slice: x: 2, y: 2, z: 4, core: 2. Of those that a mesh axis runs over, the one named last changes fastest.
Arguments:
- frames: bfloat16 [128, 4, 64, 128], P(('groups', 'date'), 'pix'), parts along dimension 0, may hold values from -6 to 6
- spatial_weight: bfloat16 [3, 3, 64, 64], P(None, None, None, 'chan'), may hold values from -0.25 to 0.25
- spatial_bias: float32 [64], P('chan'), may hold values from -3 to 3
- temporal_weight: bfloat16 [64, 64, 16], P('date', 'chan'), may hold values from -0.1875 to 0.1875
- temporal_bias: float32 [16], replicated, may hold values from -4 to 4
- head_weight: float32 [16], replicated, may hold values from -3 to 3
- labels: int32 [8, 128], P(('groups', 'pix'), ('date', 'chan')), parts along dimension 0, may hold values 0 or 1
Outputs:
- logits: float32 [8, 128], P(('groups', 'pix'), ('date', 'chan')), parts along dimension 0
- grad_spatial: float32 [6, 3, 64, 64], P('groups', None, None, 'chan'), parts along dimension 0
- grad_temporal: float32 [64, 64, 32], P('date', 'chan', 'groups'), parts along dimension 2
The draws below stay inside these ranges and needn't reach their ends.
There are 2 independent parts, one for each index of `groups`. The reference program is written for one: setup_inputs(seed, part) draws one part's arguments, and reference() takes and returns one part's arrays. A program takes and returns all parts, laid end to end along the dimension named above; an argument that names none is the same for every part. Nothing has to cross between parts.
All inputs are finite; a program needn't handle non-finite values. No bound on the sum of `labels` on one device may be relied on, other than what follows from the above.
Results may differ from the reference program's by a relative error of at most 0.024.
Values may be sent and summed in bfloat16 or wider, within the bound.
A program may use at most 64 MiB of HBM per device.

```python
import jax
import jax.numpy as jnp
from jax import lax

CHANNELS = 64
FEATURES = 16
COLS = 128
DATES = 64
HEIGHT = 4


def touch_ends(drawn, rng, low, largest):
    place = [jax.random.randint(jax.random.fold_in(rng, axis), (), 0, length) for axis, length in enumerate(drawn.shape)]
    main_axis = drawn.shape.index(max(drawn.shape))
    beside = place[:main_axis] + [(place[main_axis] + 1) % drawn.shape[main_axis]] + place[main_axis + 1:]
    return drawn.at[tuple(place)].set(low).at[tuple(beside)].set(largest)


def level_of(key, shape, cuts, smallest, top_value):
    level = 1.0
    for position, parts in cuts:
        heights = jax.random.uniform(jax.random.fold_in(jax.random.fold_in(key, 6), position), (parts,), jnp.float32, smallest / len(cuts), top_value / len(cuts))
        level = level * jnp.repeat(jnp.exp(heights), shape[position] // parts).reshape((-1,) + (1,) * (len(shape) - 1 - position))
    return level


def bell_draw(key, dims, width, most, split=(), held_as=jnp.bfloat16):
    values = width * jax.random.normal(key, dims, jnp.float32)
    if split:
        values = values * level_of(key, dims, split, -0.22, 0.18)
    return jnp.clip(values, -most, most).astype(held_as)


def setup_inputs(seed: int = 0, part: int = 0) -> dict:
    streams_of = jax.random.split(jax.random.key(seed), 8)
    own_keys = jax.random.split(jax.random.fold_in(streams_of[7], part), 8)
    frames = bell_draw(own_keys[0], (DATES, HEIGHT, CHANNELS, COLS), 1.0, 6.0, ((0, 4), (1, 2)))
    spatial_weight = bell_draw(streams_of[1], (3, 3, CHANNELS, CHANNELS), (9 * CHANNELS) ** -0.5, 0.25, ((3, 2),))
    spatial_bias = bell_draw(streams_of[2], (CHANNELS,), 0.5, 3.0, ((0, 2),), jnp.float32)
    temporal_weight = bell_draw(streams_of[3], (DATES, CHANNELS, FEATURES), (DATES * CHANNELS // 4) ** -0.5, 0.1875, ((0, 4), (1, 2)))
    temporal_bias = bell_draw(streams_of[4], (FEATURES,), 1.0, 4.0, (), jnp.float32)
    head_weight = bell_draw(streams_of[5], (FEATURES,), 0.5, 3.0, (), jnp.float32)
    labels = touch_ends((jax.random.randint(own_keys[6], (HEIGHT, COLS), 0, 3) < 1).astype(jnp.int32), jax.random.fold_in(own_keys[6], 1), 0, 1)
    return dict(frames=frames, spatial_weight=spatial_weight, spatial_bias=spatial_bias, temporal_weight=temporal_weight, temporal_bias=temporal_bias, head_weight=head_weight, labels=labels)


def spatial_preact(padded, weight, bias):
    total = jnp.zeros((HEIGHT, CHANNELS, COLS), jnp.float32) + bias[None, :, None]
    for row_off in range(3):
        for col_off in range(3):
            window = padded[row_off:row_off + HEIGHT, :, col_off:col_off + COLS].astype(jnp.float32)
            total = total + jnp.einsum('icj,co->ioj', window, weight[row_off, col_off].astype(jnp.float32))
    return total


def pad_frame(frame):
    return jnp.pad(frame, ((1, 1), (0, 0), (1, 1)))


def reference(frames, spatial_weight, spatial_bias, temporal_weight, temporal_bias, head_weight, labels):
    def forward(running, inputs):
        frame, kernel = inputs
        preact = spatial_preact(pad_frame(frame), spatial_weight, spatial_bias)
        hidden = (preact * jax.nn.sigmoid(preact)).astype(jnp.bfloat16)
        running = running + jnp.einsum('ioj,of->fij', hidden.astype(jnp.float32), kernel.astype(jnp.float32))
        return running, None

    start_sum = jnp.zeros((FEATURES, HEIGHT, COLS), jnp.float32)
    feature, unused = lax.scan(forward, start_sum, (frames, temporal_weight))
    feature = feature + temporal_bias[:, None, None]
    sigmoid_feat = jax.nn.sigmoid(feature)
    logits = jnp.einsum('fij,f->ij', feature * sigmoid_feat, head_weight)
    dlogit = jax.nn.sigmoid(logits) - labels.astype(jnp.float32)
    feature_grad = (dlogit[None] * head_weight[:, None, None] * sigmoid_feat * (1.0 + feature * (1.0 - sigmoid_feat))).astype(jnp.bfloat16)
    grad_feat = feature_grad.astype(jnp.float32)

    def backward(running, inputs):
        frame, kernel = inputs
        padded = pad_frame(frame)
        preact = spatial_preact(padded, spatial_weight, spatial_bias)
        sigmoid_pre = jax.nn.sigmoid(preact)
        hidden = (preact * sigmoid_pre).astype(jnp.bfloat16)
        temporal_part = jnp.einsum('ioj,fij->of', hidden.astype(jnp.float32), grad_feat)
        hidden_grad = jnp.einsum('fij,of->ioj', grad_feat, kernel.astype(jnp.float32))
        preact_grad = (hidden_grad * sigmoid_pre * (1.0 + preact * (1.0 - sigmoid_pre))).astype(jnp.bfloat16).astype(jnp.float32)
        rows_out = []
        for row_off in range(3):
            cols_out = []
            for col_off in range(3):
                window = padded[row_off:row_off + HEIGHT, :, col_off:col_off + COLS].astype(jnp.float32)
                cols_out.append(jnp.einsum('icj,ioj->co', window, preact_grad))
            rows_out.append(jnp.stack(cols_out))
        return running + jnp.stack(rows_out), temporal_part

    start_grad = jnp.zeros((3, 3, CHANNELS, CHANNELS), jnp.float32)
    grad_spatial, grad_temporal = lax.scan(backward, start_grad, (frames, temporal_weight))
    return logits, grad_spatial, grad_temporal
```

```python
import functools

import jax
import jax.numpy as jnp
from jax import lax
from jax.experimental import pallas as pl
from jax.experimental.pallas import tpu as pltpu
from jax.sharding import PartitionSpec as P

MESH = pl.DeviceIdType.MESH
CHUNK = 2
PIECE = 32


def fused(
    dates_n, chan_n, frames, sw, sb, tw, tb, hw, labels, logits_out, gs_out, gt_out,
    xpad, sw_v, sb_v, tw_v, tb_v, hw_v, lab_v, wbig, hid, dact, gsh,
    lab_all, feat_all, gt_all, dwb, rs_all, ag_all,
    loc_sem, halo_send, halo_recv, fwd_send, fwd_recv, lab_send, lab_recv, feat_send, feat_recv,
    gt_send, gt_recv, rs_send, rs_recv, ag_send, ag_recv,
):
    f32, bf16 = jnp.float32, jnp.bfloat16
    dates, _, channels, cols = frames.shape
    outs = sw.shape[3]
    feats = tw.shape[2]
    half = dates // chan_n
    d, p, c = lax.axis_index("date"), lax.axis_index("pix"), lax.axis_index("chan")

    def target(od, op, oc):
        return {
            "date": lax.rem(d + od, dates_n),
            "pix": lax.rem(p + op, 2),
            "chan": lax.rem(c + oc, chan_n),
        }

    def remote(src, dst, send, recv, where):
        return pltpu.make_async_remote_copy(
            src_ref=src, dst_ref=dst, send_sem=send, recv_sem=recv, device_id=where, device_id_type=MESH
        )

    barrier = pltpu.get_barrier_semaphore()
    partners = [
        (od, op, oc)
        for od in range(dates_n)
        for op in range(2)
        for oc in range(chan_n)
        if (od or op or oc) and not (op and oc)
    ]
    for offs in partners:
        pl.semaphore_signal(barrier, inc=1, device_id=target(*offs), device_id_type=MESH)

    loads = [
        pltpu.make_async_copy(src, dst, loc_sem.at[i])
        for i, (src, dst) in enumerate(
            [
                (frames, xpad.at[:, pl.ds(1, 2)]),
                (sw, sw_v),
                (sb, sb_v),
                (tw, tw_v),
                (tb, tb_v),
                (hw, hw_v),
                (labels, lab_v),
            ]
        )
    ]
    for load in loads:
        load.start()
    pl.semaphore_wait(barrier, len(partners))

    halo, passed = [], []
    for k in range(half // CHUNK):
        mine = pl.ds(c * half + k * CHUNK, CHUNK)
        halo.append(
            remote(
                frames.at[mine, 1 - p], xpad.at[mine, 3 * p], halo_send.at[k], halo_recv.at[k], target(0, 1, 0)
            )
        )
        edge = xpad.at[mine, 3 - 3 * p]
        passed.append(remote(edge, edge, fwd_send.at[k], fwd_recv.at[k], target(0, 0, 1)))
        halo[k].start()

    block = d * chan_n + c
    width = lab_v.shape[1]
    blocks = dates_n * chan_n
    group = [(od, oc) for od in reversed(range(dates_n)) for oc in reversed(range(chan_n)) if od or oc]
    loads[6].wait()
    lane = lax.broadcasted_iota(jnp.int32, (2, cols), 1)
    inside = (lane >= block * width) & (lane < (block + 1) * width)
    spread = jnp.concatenate([lab_v[...].astype(f32)] * blocks, axis=1)
    lab_all[block] = jnp.concatenate([jnp.where(inside, spread, 0.0), jnp.zeros((6, cols), f32)], axis=0)
    lab_copies = [
        remote(lab_all.at[block], lab_all.at[block], lab_send.at[n], lab_recv.at[n], target(od, 0, oc))
        for n, (od, oc) in enumerate(group)
    ]
    for copy in lab_copies:
        copy.start()

    xpad[:, 3 * p] = jnp.zeros((dates, channels, cols), bf16)
    gsh[...] = jnp.zeros(gsh.shape, bf16)
    for n in range(1, 6):
        loads[n].wait()
    wbig[...] = jnp.zeros(wbig.shape, f32)
    for a in range(3):
        for b in range(3):
            tap = sw_v[a, b].astype(f32).T
            for i in range(2):
                r = i + a
                wbig[(i * 3 + b) * outs : (i * 3 + b + 1) * outs, r * channels : (r + 1) * channels] = tap
    conv = wbig[...].astype(bf16)
    def column(row, n):
        same = lax.broadcasted_iota(jnp.int32, (n, n), 0) == lax.broadcasted_iota(jnp.int32, (n, n), 1)
        return jnp.sum(jnp.where(same, row, 0.0), axis=1, keepdims=True)
    bias_o = column(sb_v[...], outs)
    bias_f = column(tb_v[...], feats)
    head = column(hw_v[...], feats)
    tw_m = tw_v[...].reshape(dates * outs, feats)
    tw_t = tw_m.astype(f32).T.astype(bf16)
    lane_o = lax.broadcasted_iota(jnp.int32, (outs, cols), 1)
    first, last = lane_o == 0, lane_o == cols - 1

    def right(x):
        return jnp.where(first, 0.0, pltpu.roll(x, 1, 1))

    def left(x):
        return jnp.where(last, 0.0, pltpu.roll(x, cols - 1, 1))

    def forward(start):
        x = xpad[pl.ds(start, CHUNK)].reshape(CHUNK, 4 * channels, cols)
        z = jnp.dot(
            conv, jnp.concatenate([x[n] for n in range(CHUNK)], axis=1), preferred_element_type=f32
        )
        for n in range(CHUNK):
            for i in range(2):
                tap = [
                    z[(i * 3 + b) * outs : (i * 3 + b + 1) * outs, n * cols : (n + 1) * cols] for b in range(3)
                ]
                pre = tap[1] + right(tap[0]) + left(tap[2]) + bias_o
                sig = jax.nn.sigmoid(pre)
                hid[i, start + n] = (pre * sig).astype(bf16)
                dact[i, start + n] = sig * (1.0 + pre * (1.0 - sig))

    loads[0].wait()
    other = 1 - c
    steps = half // CHUNK
    for k in range(steps):
        halo[k].wait_recv()
        passed[k].start()
        forward(c * half + k * CHUNK)
        if k:
            passed[k - 1].wait_recv()
            forward(other * half + (k - 1) * CHUNK)
    passed[steps - 1].wait_recv()
    forward(other * half + (steps - 1) * CHUNK)

    hid_m = [hid[i].reshape(dates * outs, cols) for i in range(2)]
    part = jnp.concatenate([jnp.dot(tw_t, hid_m[i], preferred_element_type=f32) for i in range(2)], axis=0)
    feat_all[block] = part.astype(bf16)
    feat_copies = [
        remote(feat_all.at[block], feat_all.at[block], feat_send.at[n], feat_recv.at[n], target(od, 0, oc))
        for n, (od, oc) in enumerate(group)
    ]
    for copy in feat_copies:
        copy.start()
    for copy in lab_copies:
        copy.wait_recv()
    lab = jnp.sum(lab_all[...], axis=0)
    for copy in feat_copies:
        copy.wait_recv()
    total = jnp.sum(feat_all[...].astype(f32), axis=0)

    grads, rows_out = [], []
    for i in range(2):
        feature = total[i * feats : (i + 1) * feats] + bias_f
        sig = jax.nn.sigmoid(feature)
        logit = jnp.sum(feature * sig * head, axis=0, keepdims=True)
        dlogit = jax.nn.sigmoid(logit) - lab[i : i + 1]
        rows_out.append(logit)
        grads.append((dlogit * head * sig * (1.0 + feature * (1.0 - sig))).astype(bf16))
    fgrad = jnp.concatenate(grads, axis=1)

    contract = (((1,), (1,)), ((), ()))
    gt_all[p] = lax.dot_general(
        fgrad, jnp.concatenate(hid_m, axis=1), contract, preferred_element_type=f32
    )
    gt_copy = remote(gt_all.at[p], gt_all.at[p], gt_send, gt_recv, target(0, 1, 0))
    gt_copy.start()

    for t in range(0, dates, CHUNK):
        hgrad = jnp.dot(
            tw_m[t * outs : (t + CHUNK) * outs], fgrad, preferred_element_type=f32
        )
        for n in range(CHUNK):
            for i in range(2):
                g = hgrad[n * outs : (n + 1) * outs, i * cols : (i + 1) * cols] * dact[i, t + n]
                g = g.astype(bf16).astype(f32)
                at = slice((t + n) * cols, (t + n + 1) * cols)
                for b, v in enumerate((left(g), g, right(g))):
                    row = i * 128 + b * outs
                    gsh[row : row + outs, at] = v.astype(bf16)
    x_all = jnp.concatenate(
        [xpad[t].reshape(4 * channels, cols) for t in range(dates)], axis=1
    )
    dt = lax.dot_general(x_all, gsh[...], contract, preferred_element_type=f32)
    dwb[...] = (dt[: 3 * channels, :128] + dt[channels:, 128:]).astype(bf16)

    idx = d * 2 + p
    sums = dates_n * 2
    owners = 3 * channels // PIECE
    shift = (sums - owners) // 2
    mine = idx - shift
    is_owner = (mine >= 0) & (mine < owners)

    def rs_copy(k):
        to = {"date": (k + shift) // 2, "pix": (k + shift) % 2, "chan": c}
        return remote(
            dwb.at[pl.ds(k * PIECE, PIECE)], rs_all.at[idx], rs_send.at[k], rs_recv.at[idx], to
        )

    for k in range(owners):
        @pl.when(mine != k)
        def _():
            rs_copy(k).start()

    all_other = [(od, op) for od in reversed(range(dates_n)) for op in reversed(range(2)) if od or op]

    def ag_copies():
        return [
            remote(ag_all.at[mine], ag_all.at[mine], ag_send.at[n], ag_recv.at[mine], target(od, op, 0))
            for n, (od, op) in enumerate(all_other)
        ]

    @pl.when(is_owner)
    def _():
        rs_all[idx] = dwb[pl.ds(pl.multiple_of(mine * PIECE, PIECE), PIECE)]
        for q in range(sums):
            @pl.when(idx != q)
            def _():
                pltpu.make_async_copy(rs_all.at[q], rs_all.at[q], rs_recv.at[q]).wait()
        ag_all[mine] = jnp.sum(rs_all[...].astype(f32), axis=0).astype(bf16)
        for copy in ag_copies():
            copy.start()

    gt_copy.wait_recv()
    gt_out[...] = gt_all[0] + gt_all[1]
    logit_rows = jnp.concatenate(rows_out + [jnp.zeros((6, cols), f32)], axis=0)
    moved = pltpu.roll(logit_rows, lax.rem(cols - block * width, cols), 1)
    logits_out[...] = moved[:2, :width]
    for copy in halo + passed + lab_copies + feat_copies + [gt_copy]:
        copy.wait_send()
    for k in range(owners):
        @pl.when(mine != k)
        def _():
            rs_copy(k).wait_send()

    for k in range(owners):
        @pl.when(mine != k)
        def _():
            pltpu.make_async_copy(ag_all.at[k], ag_all.at[k], ag_recv.at[k]).wait()
        gs_out[k * PIECE : (k + 1) * PIECE] = ag_all[k].astype(f32)

    @pl.when(is_owner)
    def _():
        for copy in ag_copies():
            copy.wait_send()


def fused_shards(dates_n, chan_n, frames, sw, sb, tw, tb, hw, labels):
    dates, rows, channels, cols = frames.shape
    outs, feats = sw.shape[3], tw.shape[2]
    f32, bf16 = jnp.float32, jnp.bfloat16
    steps = dates // chan_n // CHUNK
    blocks, sums = dates_n * chan_n, dates_n * 2
    owners = 3 * channels // PIECE
    dma = pltpu.SemaphoreType.DMA
    logits, gs, gt = pl.pallas_call(
        functools.partial(fused, dates_n, chan_n),
        out_shape=(
            jax.ShapeDtypeStruct(labels.shape, f32),
            jax.ShapeDtypeStruct((3 * channels, 128), f32),
            jax.ShapeDtypeStruct((feats, dates * outs), f32),
        ),
        in_specs=[pl.BlockSpec(memory_space=pl.ANY)] * 7,
        out_specs=[pl.BlockSpec(memory_space=pltpu.VMEM)] * 3,
        scratch_shapes=[
            pltpu.VMEM((dates, 4, channels, cols), bf16),
            pltpu.VMEM(sw.shape, bf16),
            pltpu.VMEM((1, outs), f32),
            pltpu.VMEM(tw.shape, bf16),
            pltpu.VMEM((1, feats), f32),
            pltpu.VMEM((1, feats), f32),
            pltpu.VMEM(labels.shape, jnp.int32),
            pltpu.VMEM((6 * outs, 4 * channels), f32),
            pltpu.VMEM((2, dates, outs, cols), bf16),
            pltpu.VMEM((2, dates, outs, cols), f32),
            pltpu.VMEM((256, dates * cols), bf16),
            pltpu.VMEM((blocks, 8, cols), f32),
            pltpu.VMEM((blocks, 2 * feats, cols), bf16),
            pltpu.VMEM((2, feats, dates * outs), f32),
            pltpu.VMEM((3 * channels, 128), bf16),
            pltpu.VMEM((sums, PIECE, 128), bf16),
            pltpu.VMEM((owners, PIECE, 128), bf16),
            dma((7,)),
            dma((steps,)),
            dma((steps,)),
            dma((steps,)),
            dma((steps,)),
            dma((blocks,)),
            dma((blocks,)),
            dma((blocks,)),
            dma((blocks,)),
            dma,
            dma,
            dma((owners,)),
            dma((sums,)),
            dma((sums,)),
            dma((owners,)),
        ],
        compiler_params=pltpu.CompilerParams(
            collective_id=0, has_side_effects=True, vmem_limit_bytes=40 * 1024 * 1024
        ),
    )(frames, sw, sb[None], tw, tb[None], hw[None], labels)
    grad_spatial = gs[:, : 3 * outs].reshape(3, channels, 3, outs).transpose(0, 2, 1, 3)
    grad_temporal = gt.T.reshape(dates, outs, feats)
    return logits, grad_spatial, grad_temporal


def with_halo(block, sides, width):
    for axis, dim in sides:
        count = lax.axis_size(axis)
        forward = [(i, i + 1) for i in range(count - 1)]
        backward = [(target, source) for source, target in forward]
        low = lax.ppermute(
            lax.slice_in_dim(block, block.shape[dim] - width, None, axis=dim), axis, forward
        )
        high = lax.ppermute(lax.slice_in_dim(block, 0, width, axis=dim), axis, backward)
        block = jnp.concatenate([low, block, high], axis=dim)
    return block


def shards(
    frames, spatial_weight, spatial_bias, temporal_weight, temporal_bias, head_weight, labels
):
    dates_here, rows, channels, columns = frames.shape
    padded = with_halo(frames, (("pix", 1),), 1)
    padded = jnp.pad(padded, ((0, 0), (0, 0), (0, 0), (1, 1)))
    preact = spatial_bias[None, None, :, None]
    for row_off in range(3):
        for col_off in range(3):
            window = padded[:, row_off : row_off + rows, :, col_off : col_off + columns]
            preact = preact + jnp.einsum(
                "ticj,co->tioj",
                window,
                spatial_weight[row_off, col_off],
                preferred_element_type=jnp.float32,
            )
    sigmoid_pre = jax.nn.sigmoid(preact)
    hidden = (preact * sigmoid_pre).astype(jnp.bfloat16)
    partial_feat = jnp.einsum(
        "tioj,tof->fij", hidden, temporal_weight, preferred_element_type=jnp.float32
    )
    feature = (
        lax.psum_scatter(partial_feat, ("date", "chan"), scatter_dimension=2, tiled=True)
        + temporal_bias[:, None, None]
    )
    sigmoid_feat = jax.nn.sigmoid(feature)
    logits = jnp.einsum("fij,f->ij", feature * sigmoid_feat, head_weight)
    dlogit = jax.nn.sigmoid(logits) - labels.astype(jnp.float32)
    feature_grad = (
        dlogit[None]
        * head_weight[:, None, None]
        * sigmoid_feat
        * (1.0 + feature * (1.0 - sigmoid_feat))
    ).astype(jnp.bfloat16)
    full_grad = lax.all_gather(feature_grad, ("date", "chan"), axis=2, tiled=True)
    temporal_part = jnp.einsum(
        "tioj,fij->tof", hidden, full_grad, preferred_element_type=jnp.float32
    )
    hidden_grad = jnp.einsum(
        "fij,tof->tioj", full_grad, temporal_weight, preferred_element_type=jnp.float32
    )
    preact_grad = (hidden_grad * sigmoid_pre * (1.0 + preact * (1.0 - sigmoid_pre))).astype(
        jnp.bfloat16
    )
    rows_out = []
    for row_off in range(3):
        cols_out = []
        for col_off in range(3):
            window = padded[:, row_off : row_off + rows, :, col_off : col_off + columns]
            cols_out.append(
                jnp.einsum("ticj,tioj->co", window, preact_grad, preferred_element_type=jnp.float32)
            )
        rows_out.append(jnp.stack(cols_out))
    spatial_part = jnp.stack(rows_out)
    grad_temporal = lax.psum(temporal_part, "pix")
    grad_spatial = lax.psum(spatial_part, ("date", "pix"))
    return (logits, grad_spatial, grad_temporal)


def solution(mesh):
    placed = (
        P(("groups", "date"), "pix", None, None),
        P(None, None, None, "chan"),
        P("chan"),
        P("date", "chan", None),
        P(),
        P(),
        P(("groups", "pix"), ("date", "chan")),
    )
    sizes = mesh.shape
    body = shards
    if sizes["pix"] == 2 and sizes["chan"] == 2 and sizes["date"] == 4:
        body = functools.partial(fused_shards, sizes["date"], sizes["chan"])
    return jax.shard_map(
        body,
        mesh=mesh,
        in_specs=placed,
        out_specs=(
            P(("groups", "pix"), ("date", "chan")),
            P("groups", None, None, "chan"),
            P("date", "chan", "groups"),
        ),
        check_vma=False,
    )
```

```python
import functools

import jax
import jax.numpy as jnp
from jax import lax
from jax.experimental import pallas as pl
from jax.experimental.pallas import tpu as pltpu
from jax.sharding import PartitionSpec as P

MESH = pl.DeviceIdType.MESH
CHUNK = 2


def fused(
    dates_n, chan_n, frames, sw, sb, tw, tb, hw, labels, logits_out, gs_out, gt_out,
    xpad, sw_v, sb_v, tw_v, tb_v, hw_v, lab_v, wbig, tw_m, hid, dact, gsh,
    lab_all, feat_all, gt_all, dwb, rs_all, ag_all,
    loc_sem, halo_send, halo_recv, fwd_send, fwd_recv, lab_send, lab_recv, feat_send, feat_recv,
    gt_send, gt_recv, rs_send, rs_recv, ag_send, ag_recv,
):
    f32, bf16 = jnp.float32, jnp.bfloat16
    dates, _, channels, cols = frames.shape
    outs = sw.shape[2]
    feats = tw.shape[1]
    half = dates // chan_n
    d, p, c = lax.axis_index("date"), lax.axis_index("pix"), lax.axis_index("chan")

    def target(od, op, oc):
        return {
            "date": lax.rem(d + od, dates_n),
            "pix": lax.rem(p + op, 2),
            "chan": lax.rem(c + oc, chan_n),
        }

    def remote(src, dst, send, recv, where):
        return pltpu.make_async_remote_copy(
            src_ref=src, dst_ref=dst, send_sem=send, recv_sem=recv, device_id=where, device_id_type=MESH
        )

    barrier = pltpu.get_barrier_semaphore()
    partners = [
        (od, op, oc)
        for od in range(dates_n)
        for op in range(2)
        for oc in range(chan_n)
        if (od or op or oc) and not (op and oc)
    ]
    for offs in partners:
        pl.semaphore_signal(barrier, inc=1, device_id=target(*offs), device_id_type=MESH)

    loads = [
        pltpu.make_async_copy(src, dst, loc_sem.at[i])
        for i, (src, dst) in enumerate(
            [
                (frames, xpad.at[:, pl.ds(1, 2)]),
                (sw, sw_v),
                (sb, sb_v),
                (tw, tw_v),
                (tb, tb_v),
                (hw, hw_v),
                (labels, lab_v),
            ]
        )
    ]
    for load in loads:
        load.start()
    pl.semaphore_wait(barrier, len(partners))

    halo, passed = [], []
    for k in range(half // CHUNK):
        mine = pl.ds(c * half + k * CHUNK, CHUNK)
        halo.append(
            remote(
                frames.at[mine, 1 - p], xpad.at[mine, 3 * p], halo_send.at[k], halo_recv.at[k], target(0, 1, 0)
            )
        )
        edge = xpad.at[mine, 3 - 3 * p]
        passed.append(remote(edge, edge, fwd_send.at[k], fwd_recv.at[k], target(0, 0, 1)))
        halo[k].start()

    block = d * chan_n + c
    width = lab_v.shape[1]
    blocks = dates_n * chan_n
    group = [(od, oc) for od in reversed(range(dates_n)) for oc in reversed(range(chan_n)) if od or oc]
    loads[6].wait()
    lane = lax.broadcasted_iota(jnp.int32, (2, cols), 1)
    inside = (lane >= block * width) & (lane < (block + 1) * width)
    spread = jnp.concatenate([lab_v[...].astype(f32)] * blocks, axis=1)
    lab_all[block] = jnp.concatenate([jnp.where(inside, spread, 0.0), jnp.zeros((6, cols), f32)], axis=0)
    lab_copies = [
        remote(lab_all.at[block], lab_all.at[block], lab_send.at[n], lab_recv.at[n], target(od, 0, oc))
        for n, (od, oc) in enumerate(group)
    ]
    for copy in lab_copies:
        copy.start()

    xpad[:, 3 * p] = jnp.zeros((dates, channels, cols), bf16)
    for n in range(1, 6):
        loads[n].wait()
    wbig[...] = jnp.zeros(wbig.shape, f32)
    for a in range(3):
        for b in range(3):
            tap = sw_v[a, b].astype(f32)
            for i in range(2):
                r = i + a
                wbig[(i * 3 + b) * outs : (i * 3 + b + 1) * outs, r * channels : (r + 1) * channels] = tap
    conv = wbig[...].astype(bf16)
    def column(row, n):
        same = lax.broadcasted_iota(jnp.int32, (n, n), 0) == lax.broadcasted_iota(jnp.int32, (n, n), 1)
        return jnp.sum(jnp.where(same, row, 0.0), axis=1, keepdims=True)
    bias_o = column(sb_v[...], outs)
    bias_f = column(tb_v[...], feats)
    head = column(hw_v[...], feats)
    tw_f = jnp.concatenate([tw_v[t].astype(f32) for t in range(dates)], axis=1)
    tw_t = tw_f.astype(bf16)
    tw_m[...] = tw_f.T.astype(bf16)
    lane_o = lax.broadcasted_iota(jnp.int32, (outs, cols), 1)
    first, last = lane_o == 0, lane_o == cols - 1

    def right(x):
        return jnp.where(first, 0.0, pltpu.roll(x, 1, 1))

    def left(x):
        return jnp.where(last, 0.0, pltpu.roll(x, cols - 1, 1))

    def forward(start):
        x = xpad[pl.ds(start, CHUNK)].reshape(CHUNK, 4 * channels, cols)
        z = jnp.dot(
            conv, jnp.concatenate([x[n] for n in range(CHUNK)], axis=1), preferred_element_type=f32
        )
        for n in range(CHUNK):
            for i in range(2):
                tap = [
                    z[(i * 3 + b) * outs : (i * 3 + b + 1) * outs, n * cols : (n + 1) * cols] for b in range(3)
                ]
                pre = tap[1] + right(tap[0]) + left(tap[2]) + bias_o
                sig = jax.nn.sigmoid(pre)
                hid[i, start + n] = (pre * sig).astype(bf16)
                dact[i, start + n] = sig * (1.0 + pre * (1.0 - sig))

    loads[0].wait()
    other = 1 - c
    steps = half // CHUNK
    for k in range(steps):
        halo[k].wait_recv()
        passed[k].start()
        forward(c * half + k * CHUNK)
        if k:
            passed[k - 1].wait_recv()
            forward(other * half + (k - 1) * CHUNK)
    passed[steps - 1].wait_recv()
    forward(other * half + (steps - 1) * CHUNK)

    hid_m = [hid[i].reshape(dates * outs, cols) for i in range(2)]
    part = jnp.concatenate([jnp.dot(tw_t, hid_m[i], preferred_element_type=f32) for i in range(2)], axis=0)
    feat_all[block] = part.astype(bf16)
    feat_copies = [
        remote(feat_all.at[block], feat_all.at[block], feat_send.at[n], feat_recv.at[n], target(od, 0, oc))
        for n, (od, oc) in enumerate(group)
    ]
    for copy in feat_copies:
        copy.start()
    for copy in lab_copies:
        copy.wait_recv()
    lab = jnp.sum(lab_all[...], axis=0)
    for copy in feat_copies:
        copy.wait_recv()
    total = jnp.sum(feat_all[...].astype(f32), axis=0)

    grads, rows_out = [], []
    for i in range(2):
        feature = total[i * feats : (i + 1) * feats] + bias_f
        sig = jax.nn.sigmoid(feature)
        logit = jnp.sum(feature * sig * head, axis=0, keepdims=True)
        dlogit = jax.nn.sigmoid(logit) - lab[i : i + 1]
        rows_out.append(logit)
        grads.append((dlogit * head * sig * (1.0 + feature * (1.0 - sig))).astype(bf16))
    fgrad = jnp.concatenate(grads, axis=1)

    contract = (((1,), (1,)), ((), ()))
    gt_all[p] = lax.dot_general(
        fgrad, jnp.concatenate(hid_m, axis=1), contract, preferred_element_type=f32
    )
    gt_copy = remote(gt_all.at[p], gt_all.at[p], gt_send, gt_recv, target(0, 1, 0))
    gt_copy.start()

    for t in range(0, dates, CHUNK):
        hgrad = jnp.dot(
            tw_m[t * outs : (t + CHUNK) * outs], fgrad, preferred_element_type=f32
        )
        for n in range(CHUNK):
            for i in range(2):
                g = hgrad[n * outs : (n + 1) * outs, i * cols : (i + 1) * cols] * dact[i, t + n]
                g = g.astype(bf16).astype(f32)
                at = slice((t + n) * cols, (t + n + 1) * cols)
                for b, v in enumerate((left(g), g, right(g))):
                    row = (i * 3 + b) * outs
                    gsh[row : row + outs, at] = v.astype(bf16)
    x_all = jnp.concatenate(
        [xpad[t].reshape(4 * channels, cols) for t in range(dates)], axis=1
    )
    dt = lax.dot_general(gsh[...], x_all, contract, preferred_element_type=f32)
    dw = dt[: 3 * outs] + pltpu.roll(dt[3 * outs :], 3 * channels, 1)
    for b in range(3):
        for h in range(2):
            dwb[2 * b + h] = dw[b * outs : (b + 1) * outs, h * 128 : (h + 1) * 128].astype(bf16)

    idx = d * 2 + p
    sums = dates_n * 2
    owners = dwb.shape[0]
    shift = (sums - owners) // 2
    mine = idx - shift
    is_owner = (mine >= 0) & (mine < owners)

    def rs_copy(k):
        to = {"date": (k + shift) // 2, "pix": (k + shift) % 2, "chan": c}
        return remote(
            dwb.at[k], rs_all.at[idx], rs_send.at[k], rs_recv.at[idx], to
        )

    for k in range(owners):
        @pl.when(mine != k)
        def _():
            rs_copy(k).start()

    all_other = [(od, op) for od in reversed(range(dates_n)) for op in reversed(range(2)) if od or op]

    def ag_copies():
        return [
            remote(ag_all.at[mine], ag_all.at[mine], ag_send.at[n], ag_recv.at[mine], target(od, op, 0))
            for n, (od, op) in enumerate(all_other)
        ]

    @pl.when(is_owner)
    def _():
        rs_all[idx] = dwb[mine]
        for q in range(sums):
            @pl.when(idx != q)
            def _():
                pltpu.make_async_copy(rs_all.at[q], rs_all.at[q], rs_recv.at[q]).wait()
        ag_all[mine] = jnp.sum(rs_all[...].astype(f32), axis=0).astype(bf16)
        for copy in ag_copies():
            copy.start()

    gt_copy.wait_recv()
    for t in range(dates):
        at = slice(t * outs, (t + 1) * outs)
        gt_out[t] = gt_all[0, :, at] + gt_all[1, :, at]
    logit_rows = jnp.concatenate(rows_out + [jnp.zeros((6, cols), f32)], axis=0)
    moved = pltpu.roll(logit_rows, lax.rem(cols - block * width, cols), 1)
    logits_out[...] = moved[:2, :width]
    for copy in halo + passed + lab_copies + feat_copies + [gt_copy]:
        copy.wait_send()
    for k in range(owners):
        @pl.when(mine != k)
        def _():
            rs_copy(k).wait_send()

    for k in range(owners):
        @pl.when(mine != k)
        def _():
            pltpu.make_async_copy(ag_all.at[k], ag_all.at[k], ag_recv.at[k]).wait()
        piece = ag_all[k].astype(f32)
        for n in range(2 - k % 2):
            gs_out[2 * (k % 2) + n, k // 2] = piece[:, n * channels : (n + 1) * channels]

    @pl.when(is_owner)
    def _():
        for copy in ag_copies():
            copy.wait_send()


def store(*refs):
    sem = refs[6]
    copies = [pltpu.make_async_copy(refs[i], refs[3 + i], sem.at[i]) for i in range(3)]
    for copy in copies:
        copy.start()
    for copy in copies:
        copy.wait()


def fused_shards(dates_n, chan_n, frames, sw, sb, tw, tb, hw, labels):
    dates, rows, channels, cols = frames.shape
    outs, feats = sw.shape[3], tw.shape[2]
    sw, tw = sw.transpose(0, 1, 3, 2), tw.transpose(0, 2, 1)
    f32, bf16 = jnp.float32, jnp.bfloat16
    steps = dates // chan_n // CHUNK
    blocks, sums = dates_n * chan_n, dates_n * 2
    owners = 6
    dma = pltpu.SemaphoreType.DMA
    made = pl.pallas_call(
        functools.partial(fused, dates_n, chan_n),
        out_shape=(
            jax.ShapeDtypeStruct(labels.shape, f32),
            jax.ShapeDtypeStruct(sw.shape, f32),
            jax.ShapeDtypeStruct(tw.shape, f32),
        ),
        in_specs=[pl.BlockSpec(memory_space=pltpu.HBM)] * 7,
        out_specs=[pl.BlockSpec(memory_space=pltpu.VMEM)] * 3,
        scratch_shapes=[
            pltpu.VMEM((dates, 4, channels, cols), bf16),
            pltpu.VMEM(sw.shape, bf16),
            pltpu.VMEM((1, outs), f32),
            pltpu.VMEM(tw.shape, bf16),
            pltpu.VMEM((1, feats), f32),
            pltpu.VMEM((1, feats), f32),
            pltpu.VMEM(labels.shape, jnp.int32),
            pltpu.VMEM((6 * outs, 4 * channels), f32),
            pltpu.VMEM((dates * outs, feats), bf16),
            pltpu.VMEM((2, dates, outs, cols), bf16),
            pltpu.VMEM((2, dates, outs, cols), f32),
            pltpu.VMEM((6 * outs, dates * cols), bf16),
            pltpu.VMEM((blocks, 8, cols), f32),
            pltpu.VMEM((blocks, 2 * feats, cols), bf16),
            pltpu.VMEM((2, feats, dates * outs), f32),
            pltpu.VMEM((owners, outs, 128), bf16),
            pltpu.VMEM((sums, outs, 128), bf16),
            pltpu.VMEM((owners, outs, 128), bf16),
            dma((7,)),
            dma((steps,)),
            dma((steps,)),
            dma((steps,)),
            dma((steps,)),
            dma((blocks,)),
            dma((blocks,)),
            dma((blocks,)),
            dma((blocks,)),
            dma,
            dma,
            dma((owners,)),
            dma((sums,)),
            dma((sums,)),
            dma((owners,)),
        ],
        compiler_params=pltpu.CompilerParams(
            collective_id=0, has_side_effects=True, vmem_limit_bytes=56_000_000
        ),
    )(frames, sw, sb[None], tw, tb[None], hw[None], labels)
    logits, gs, gt = pl.pallas_call(
        store,
        out_shape=tuple(jax.ShapeDtypeStruct(a.shape, a.dtype) for a in made),
        in_specs=[pl.BlockSpec(memory_space=pl.ANY)] * 3,
        out_specs=[pl.BlockSpec(memory_space=pl.ANY)] * 3,
        scratch_shapes=[dma((3,))],
        compiler_params=pltpu.CompilerParams(vmem_limit_bytes=1 << 20),
    )(*made)
    return logits, gs.transpose(0, 1, 3, 2), gt.transpose(0, 2, 1)


def with_halo(block, sides, width):
    for axis, dim in sides:
        count = lax.axis_size(axis)
        forward = [(i, i + 1) for i in range(count - 1)]
        backward = [(target, source) for source, target in forward]
        low = lax.ppermute(
            lax.slice_in_dim(block, block.shape[dim] - width, None, axis=dim), axis, forward
        )
        high = lax.ppermute(lax.slice_in_dim(block, 0, width, axis=dim), axis, backward)
        block = jnp.concatenate([low, block, high], axis=dim)
    return block


def shards(
    frames, spatial_weight, spatial_bias, temporal_weight, temporal_bias, head_weight, labels
):
    dates_here, rows, channels, columns = frames.shape
    padded = with_halo(frames, (("pix", 1),), 1)
    padded = jnp.pad(padded, ((0, 0), (0, 0), (0, 0), (1, 1)))
    preact = spatial_bias[None, None, :, None]
    for row_off in range(3):
        for col_off in range(3):
            window = padded[:, row_off : row_off + rows, :, col_off : col_off + columns]
            preact = preact + jnp.einsum(
                "ticj,co->tioj",
                window,
                spatial_weight[row_off, col_off],
                preferred_element_type=jnp.float32,
            )
    sigmoid_pre = jax.nn.sigmoid(preact)
    hidden = (preact * sigmoid_pre).astype(jnp.bfloat16)
    partial_feat = jnp.einsum(
        "tioj,tof->fij", hidden, temporal_weight, preferred_element_type=jnp.float32
    )
    feature = (
        lax.psum_scatter(partial_feat, ("date", "chan"), scatter_dimension=2, tiled=True)
        + temporal_bias[:, None, None]
    )
    sigmoid_feat = jax.nn.sigmoid(feature)
    logits = jnp.einsum("fij,f->ij", feature * sigmoid_feat, head_weight)
    dlogit = jax.nn.sigmoid(logits) - labels.astype(jnp.float32)
    feature_grad = (
        dlogit[None]
        * head_weight[:, None, None]
        * sigmoid_feat
        * (1.0 + feature * (1.0 - sigmoid_feat))
    ).astype(jnp.bfloat16)
    full_grad = lax.all_gather(feature_grad, ("date", "chan"), axis=2, tiled=True)
    temporal_part = jnp.einsum(
        "tioj,fij->tof", hidden, full_grad, preferred_element_type=jnp.float32
    )
    hidden_grad = jnp.einsum(
        "fij,tof->tioj", full_grad, temporal_weight, preferred_element_type=jnp.float32
    )
    preact_grad = (hidden_grad * sigmoid_pre * (1.0 + preact * (1.0 - sigmoid_pre))).astype(
        jnp.bfloat16
    )
    rows_out = []
    for row_off in range(3):
        cols_out = []
        for col_off in range(3):
            window = padded[:, row_off : row_off + rows, :, col_off : col_off + columns]
            cols_out.append(
                jnp.einsum("ticj,tioj->co", window, preact_grad, preferred_element_type=jnp.float32)
            )
        rows_out.append(jnp.stack(cols_out))
    spatial_part = jnp.stack(rows_out)
    grad_temporal = lax.psum(temporal_part, "pix")
    grad_spatial = lax.psum(spatial_part, ("date", "pix"))
    return (logits, grad_spatial, grad_temporal)


def solution(mesh):
    placed = (
        P(("groups", "date"), "pix", None, None),
        P(None, None, None, "chan"),
        P("chan"),
        P("date", "chan", None),
        P(),
        P(),
        P(("groups", "pix"), ("date", "chan")),
    )
    sizes = mesh.shape
    body = shards
    if sizes["pix"] == 2 and sizes["chan"] == 2 and sizes["date"] == 4:
        body = functools.partial(fused_shards, sizes["date"], sizes["chan"])
    return jax.shard_map(
        body,
        mesh=mesh,
        in_specs=placed,
        out_specs=(
            P(("groups", "pix"), ("date", "chan")),
            P("groups", None, None, "chan"),
            P("date", "chan", "groups"),
        ),
        check_vma=False,
    )
```

```python
import functools

import jax
import jax.numpy as jnp
from jax import lax
from jax.experimental import pallas as pl
from jax.experimental.pallas import tpu as pltpu
from jax.sharding import PartitionSpec as P

MESH = pl.DeviceIdType.MESH
CHUNK = 8


def fused(
    dates_n, chan_n, frames, sw, sb, tw, tb, hw, labels, logits_out, gs_out, gt_out,
    xpad, sw_v, sb_v, tw_v, tb_v, hw_v, lab_v, wbig, tw_m, hid, dact, gsh,
    lab_all, feat_all, gt_all, dwb, rs_all, ag_all,
    loc_sem, halo_send, halo_recv, fwd_send, fwd_recv, lab_send, lab_recv, feat_send, feat_recv,
    gt_send, gt_recv, rs_send, rs_recv, ag_send, ag_recv,
):
    f32, bf16 = jnp.float32, jnp.bfloat16
    dates, _, channels, cols = frames.shape
    outs = sw.shape[2]
    feats = tw.shape[1]
    half = dates // chan_n
    d, p, c = lax.axis_index("date"), lax.axis_index("pix"), lax.axis_index("chan")

    def target(od, op, oc):
        return {
            "date": lax.rem(d + od, dates_n),
            "pix": lax.rem(p + op, 2),
            "chan": lax.rem(c + oc, chan_n),
        }

    def remote(src, dst, send, recv, where):
        return pltpu.make_async_remote_copy(
            src_ref=src, dst_ref=dst, send_sem=send, recv_sem=recv, device_id=where, device_id_type=MESH
        )

    barrier = pltpu.get_barrier_semaphore()
    partners = [
        (od, op, oc)
        for od in range(dates_n)
        for op in range(2)
        for oc in range(chan_n)
        if (od or op or oc) and not (op and oc)
    ]
    for offs in partners:
        pl.semaphore_signal(barrier, inc=1, device_id=target(*offs), device_id_type=MESH)

    loads = [
        pltpu.make_async_copy(src, dst, loc_sem.at[i])
        for i, (src, dst) in enumerate(
            [
                (frames, xpad.at[:, pl.ds(1, 2)]),
                (sw, sw_v),
                (sb, sb_v),
                (tw, tw_v),
                (tb, tb_v),
                (hw, hw_v),
                (labels, lab_v),
            ]
        )
    ]
    for load in loads:
        load.start()
    pl.semaphore_wait(barrier, len(partners))

    halo, passed = [], []
    for k in range(half // CHUNK):
        mine = pl.ds(c * half + k * CHUNK, CHUNK)
        halo.append(
            remote(
                frames.at[mine, 1 - p], xpad.at[mine, 3 * p], halo_send.at[k], halo_recv.at[k], target(0, 1, 0)
            )
        )
        edge = xpad.at[mine, 3 - 3 * p]
        passed.append(remote(edge, edge, fwd_send.at[k], fwd_recv.at[k], target(0, 0, 1)))
        halo[k].start()

    block = d * chan_n + c
    width = lab_v.shape[1]
    blocks = dates_n * chan_n
    group = [(od, oc) for od in reversed(range(dates_n)) for oc in reversed(range(chan_n)) if od or oc]
    loads[6].wait()
    lane = lax.broadcasted_iota(jnp.int32, (2, cols), 1)
    inside = (lane >= block * width) & (lane < (block + 1) * width)
    spread = jnp.concatenate([lab_v[...].astype(f32)] * blocks, axis=1)
    lab_all[block] = jnp.concatenate([jnp.where(inside, spread, 0.0), jnp.zeros((6, cols), f32)], axis=0)
    lab_copies = [
        remote(lab_all.at[block], lab_all.at[block], lab_send.at[n], lab_recv.at[n], target(od, 0, oc))
        for n, (od, oc) in enumerate(group)
    ]
    for copy in lab_copies:
        copy.start()

    xpad[:, 3 * p] = jnp.zeros((dates, channels, cols), bf16)
    for n in range(1, 6):
        loads[n].wait()
    wbig[...] = jnp.zeros(wbig.shape, f32)
    for a in range(3):
        for b in range(3):
            tap = sw_v[a, b].astype(f32)
            for i in range(2):
                r = i + a
                wbig[(i * 3 + b) * outs : (i * 3 + b + 1) * outs, r * channels : (r + 1) * channels] = tap
    conv = wbig[...].astype(bf16)
    def column(row, n):
        same = lax.broadcasted_iota(jnp.int32, (n, n), 0) == lax.broadcasted_iota(jnp.int32, (n, n), 1)
        return jnp.sum(jnp.where(same, row, 0.0), axis=1, keepdims=True)
    bias_o = column(sb_v[...], outs)
    bias_f = column(tb_v[...], feats)
    head = column(hw_v[...], feats)
    tw_f = jnp.concatenate([tw_v[t].astype(f32) for t in range(dates)], axis=1)
    tw_t = tw_f.astype(bf16)
    tw_m[...] = tw_f.T.astype(bf16)
    lane_o = lax.broadcasted_iota(jnp.int32, (outs, cols), 1)
    first, last = lane_o == 0, lane_o == cols - 1

    def right(x):
        return jnp.where(first, 0.0, pltpu.roll(x, 1, 1))

    def left(x):
        return jnp.where(last, 0.0, pltpu.roll(x, cols - 1, 1))

    def forward(start):
        x = xpad[pl.ds(start, CHUNK)].reshape(CHUNK, 4 * channels, cols)
        z = jnp.dot(
            conv, jnp.concatenate([x[n] for n in range(CHUNK)], axis=1), preferred_element_type=f32
        )
        for n in range(CHUNK):
            for i in range(2):
                tap = [
                    z[(i * 3 + b) * outs : (i * 3 + b + 1) * outs, n * cols : (n + 1) * cols] for b in range(3)
                ]
                pre = tap[1] + right(tap[0]) + left(tap[2]) + bias_o
                sig = jax.nn.sigmoid(pre)
                hid[i, start + n] = (pre * sig).astype(bf16)
                dact[i, start + n] = sig * (1.0 + pre * (1.0 - sig))

    loads[0].wait()
    other = 1 - c
    steps = half // CHUNK
    for k in range(steps):
        halo[k].wait_recv()
        passed[k].start()
        forward(c * half + k * CHUNK)
        if k:
            passed[k - 1].wait_recv()
            forward(other * half + (k - 1) * CHUNK)
    passed[steps - 1].wait_recv()
    forward(other * half + (steps - 1) * CHUNK)

    hid_m = [hid[i].reshape(dates * outs, cols) for i in range(2)]
    part = jnp.concatenate([jnp.dot(tw_t, hid_m[i], preferred_element_type=f32) for i in range(2)], axis=0)
    feat_all[block] = part.astype(bf16)
    feat_copies = [
        remote(feat_all.at[block], feat_all.at[block], feat_send.at[n], feat_recv.at[n], target(od, 0, oc))
        for n, (od, oc) in enumerate(group)
    ]
    for copy in feat_copies:
        copy.start()
    for copy in lab_copies:
        copy.wait_recv()
    lab = jnp.sum(lab_all[...], axis=0)
    for copy in feat_copies:
        copy.wait_recv()
    total = jnp.sum(feat_all[...].astype(f32), axis=0)

    grads, rows_out = [], []
    for i in range(2):
        feature = total[i * feats : (i + 1) * feats] + bias_f
        sig = jax.nn.sigmoid(feature)
        logit = jnp.sum(feature * sig * head, axis=0, keepdims=True)
        dlogit = jax.nn.sigmoid(logit) - lab[i : i + 1]
        rows_out.append(logit)
        grads.append((dlogit * head * sig * (1.0 + feature * (1.0 - sig))).astype(bf16))
    fgrad = jnp.concatenate(grads, axis=1)

    contract = (((1,), (1,)), ((), ()))

    for t in range(0, dates, CHUNK):
        hgrad = jnp.dot(
            tw_m[t * outs : (t + CHUNK) * outs], fgrad, preferred_element_type=f32
        )
        for n in range(CHUNK):
            for i in range(2):
                g = hgrad[n * outs : (n + 1) * outs, i * cols : (i + 1) * cols] * dact[i, t + n]
                g = g.astype(bf16).astype(f32)
                at = slice((t + n) * cols, (t + n + 1) * cols)
                for b, v in enumerate((left(g), g, right(g))):
                    row = (i * 3 + b) * outs
                    gsh[row : row + outs, at] = v.astype(bf16)
    x_all = jnp.concatenate(
        [xpad[t].reshape(4 * channels, cols) for t in range(dates)], axis=1
    )
    dt = lax.dot_general(gsh[...], x_all, contract, preferred_element_type=f32)
    dw = dt[: 3 * outs] + pltpu.roll(dt[3 * outs :], 3 * channels, 1)
    for b in range(3):
        for h in range(2):
            dwb[2 * b + h] = dw[b * outs : (b + 1) * outs, h * 128 : (h + 1) * 128].astype(bf16)

    idx = d * 2 + p
    sums = dates_n * 2
    owners = dwb.shape[0]
    shift = (sums - owners) // 2
    mine = idx - shift
    is_owner = (mine >= 0) & (mine < owners)

    def rs_copy(k):
        to = {"date": (k + shift) // 2, "pix": (k + shift) % 2, "chan": c}
        return remote(
            dwb.at[k], rs_all.at[idx], rs_send.at[k], rs_recv.at[idx], to
        )

    for k in range(owners):
        @pl.when(mine != k)
        def _():
            rs_copy(k).start()

    gt_all[p] = lax.dot_general(
        fgrad, jnp.concatenate(hid_m, axis=1), contract, preferred_element_type=f32
    )
    gt_copy = remote(gt_all.at[p], gt_all.at[p], gt_send, gt_recv, target(0, 1, 0))
    gt_copy.start()

    all_other = [(od, op) for od in reversed(range(dates_n)) for op in reversed(range(2)) if od or op]

    def ag_copies():
        return [
            remote(ag_all.at[mine], ag_all.at[mine], ag_send.at[n], ag_recv.at[mine], target(od, op, 0))
            for n, (od, op) in enumerate(all_other)
        ]

    @pl.when(is_owner)
    def _():
        rs_all[idx] = dwb[mine]
        for q in range(sums):
            @pl.when(idx != q)
            def _():
                pltpu.make_async_copy(rs_all.at[q], rs_all.at[q], rs_recv.at[q]).wait()
        ag_all[mine] = jnp.sum(rs_all[...].astype(f32), axis=0).astype(bf16)
        for copy in ag_copies():
            copy.start()

    gt_copy.wait_recv()
    gt_out[...] = gt_all[0] + gt_all[1]
    logit_rows = jnp.concatenate(rows_out + [jnp.zeros((6, cols), f32)], axis=0)
    moved = pltpu.roll(logit_rows, lax.rem(cols - block * width, cols), 1)
    logits_out[...] = moved[:2, :width]
    for copy in halo + passed + lab_copies + feat_copies + [gt_copy]:
        copy.wait_send()
    for k in range(owners):
        @pl.when(mine != k)
        def _():
            rs_copy(k).wait_send()

    for k in range(owners):
        @pl.when(mine != k)
        def _():
            pltpu.make_async_copy(ag_all.at[k], ag_all.at[k], ag_recv.at[k]).wait()
        gs_out[k] = ag_all[k]

    @pl.when(is_owner)
    def _():
        for copy in ag_copies():
            copy.wait_send()


def unpack(logits, gs, gt, logits_out, gs_out, gt_out):
    channels = gs_out.shape[3]
    outs = gt_out.shape[2]
    logits_out[...] = logits[...]
    for k in range(gs.shape[0]):
        piece = gs[k].astype(jnp.float32)
        for n in range(2 - k % 2):
            gs_out[2 * (k % 2) + n, k // 2] = piece[:, n * channels : (n + 1) * channels]
    for t in range(gt_out.shape[0]):
        gt_out[t] = gt[:, t * outs : (t + 1) * outs]


def fused_shards(dates_n, chan_n, frames, sw, sb, tw, tb, hw, labels):
    dates, rows, channels, cols = frames.shape
    outs, feats = sw.shape[3], tw.shape[2]
    sw, tw = sw.transpose(0, 1, 3, 2), tw.transpose(0, 2, 1)
    f32, bf16 = jnp.float32, jnp.bfloat16
    steps = dates // chan_n // CHUNK
    blocks, sums = dates_n * chan_n, dates_n * 2
    owners = 6
    dma = pltpu.SemaphoreType.DMA
    made = pl.pallas_call(
        functools.partial(fused, dates_n, chan_n),
        out_shape=(
            jax.ShapeDtypeStruct(labels.shape, f32),
            jax.ShapeDtypeStruct((owners, outs, 128), bf16),
            jax.ShapeDtypeStruct((feats, dates * outs), f32),
        ),
        in_specs=[pl.BlockSpec(memory_space=pltpu.HBM)] * 7,
        out_specs=[pl.BlockSpec(memory_space=pltpu.VMEM)] * 3,
        scratch_shapes=[
            pltpu.VMEM((dates, 4, channels, cols), bf16),
            pltpu.VMEM(sw.shape, bf16),
            pltpu.VMEM((1, outs), f32),
            pltpu.VMEM(tw.shape, bf16),
            pltpu.VMEM((1, feats), f32),
            pltpu.VMEM((1, feats), f32),
            pltpu.VMEM(labels.shape, jnp.int32),
            pltpu.VMEM((6 * outs, 4 * channels), f32),
            pltpu.VMEM((dates * outs, feats), bf16),
            pltpu.VMEM((2, dates, outs, cols), bf16),
            pltpu.VMEM((2, dates, outs, cols), f32),
            pltpu.VMEM((6 * outs, dates * cols), bf16),
            pltpu.VMEM((blocks, 8, cols), f32),
            pltpu.VMEM((blocks, 2 * feats, cols), bf16),
            pltpu.VMEM((2, feats, dates * outs), f32),
            pltpu.VMEM((owners, outs, 128), bf16),
            pltpu.VMEM((sums, outs, 128), bf16),
            pltpu.VMEM((owners, outs, 128), bf16),
            dma((7,)),
            dma((steps,)),
            dma((steps,)),
            dma((steps,)),
            dma((steps,)),
            dma((blocks,)),
            dma((blocks,)),
            dma((blocks,)),
            dma((blocks,)),
            dma,
            dma,
            dma((owners,)),
            dma((sums,)),
            dma((sums,)),
            dma((owners,)),
        ],
        compiler_params=pltpu.CompilerParams(
            collective_id=0, has_side_effects=True, vmem_limit_bytes=56_400_000
        ),
    )(frames, sw, sb[None], tw, tb[None], hw[None], labels)
    logits, gs, gt = pl.pallas_call(
        unpack,
        out_shape=tuple(jax.ShapeDtypeStruct(shape, f32) for shape in (labels.shape, sw.shape, tw.shape)),
        in_specs=[pl.BlockSpec(memory_space=pltpu.VMEM)] * 3,
        out_specs=[pl.BlockSpec(memory_space=pltpu.VMEM)] * 3,
        compiler_params=pltpu.CompilerParams(vmem_limit_bytes=1 << 20),
    )(*made)
    return logits, gs.transpose(0, 1, 3, 2), gt.transpose(0, 2, 1)


def with_halo(block, sides, width):
    for axis, dim in sides:
        count = lax.axis_size(axis)
        forward = [(i, i + 1) for i in range(count - 1)]
        backward = [(target, source) for source, target in forward]
        low = lax.ppermute(
            lax.slice_in_dim(block, block.shape[dim] - width, None, axis=dim), axis, forward
        )
        high = lax.ppermute(lax.slice_in_dim(block, 0, width, axis=dim), axis, backward)
        block = jnp.concatenate([low, block, high], axis=dim)
    return block


def shards(
    frames, spatial_weight, spatial_bias, temporal_weight, temporal_bias, head_weight, labels
):
    dates_here, rows, channels, columns = frames.shape
    padded = with_halo(frames, (("pix", 1),), 1)
    padded = jnp.pad(padded, ((0, 0), (0, 0), (0, 0), (1, 1)))
    preact = spatial_bias[None, None, :, None]
    for row_off in range(3):
        for col_off in range(3):
            window = padded[:, row_off : row_off + rows, :, col_off : col_off + columns]
            preact = preact + jnp.einsum(
                "ticj,co->tioj",
                window,
                spatial_weight[row_off, col_off],
                preferred_element_type=jnp.float32,
            )
    sigmoid_pre = jax.nn.sigmoid(preact)
    hidden = (preact * sigmoid_pre).astype(jnp.bfloat16)
    partial_feat = jnp.einsum(
        "tioj,tof->fij", hidden, temporal_weight, preferred_element_type=jnp.float32
    )
    feature = (
        lax.psum_scatter(partial_feat, ("date", "chan"), scatter_dimension=2, tiled=True)
        + temporal_bias[:, None, None]
    )
    sigmoid_feat = jax.nn.sigmoid(feature)
    logits = jnp.einsum("fij,f->ij", feature * sigmoid_feat, head_weight)
    dlogit = jax.nn.sigmoid(logits) - labels.astype(jnp.float32)
    feature_grad = (
        dlogit[None]
        * head_weight[:, None, None]
        * sigmoid_feat
        * (1.0 + feature * (1.0 - sigmoid_feat))
    ).astype(jnp.bfloat16)
    full_grad = lax.all_gather(feature_grad, ("date", "chan"), axis=2, tiled=True)
    temporal_part = jnp.einsum(
        "tioj,fij->tof", hidden, full_grad, preferred_element_type=jnp.float32
    )
    hidden_grad = jnp.einsum(
        "fij,tof->tioj", full_grad, temporal_weight, preferred_element_type=jnp.float32
    )
    preact_grad = (hidden_grad * sigmoid_pre * (1.0 + preact * (1.0 - sigmoid_pre))).astype(
        jnp.bfloat16
    )
    rows_out = []
    for row_off in range(3):
        cols_out = []
        for col_off in range(3):
            window = padded[:, row_off : row_off + rows, :, col_off : col_off + columns]
            cols_out.append(
                jnp.einsum("ticj,tioj->co", window, preact_grad, preferred_element_type=jnp.float32)
            )
        rows_out.append(jnp.stack(cols_out))
    spatial_part = jnp.stack(rows_out)
    grad_temporal = lax.psum(temporal_part, "pix")
    grad_spatial = lax.psum(spatial_part, ("date", "pix"))
    return (logits, grad_spatial, grad_temporal)


def solution(mesh):
    placed = (
        P(("groups", "date"), "pix", None, None),
        P(None, None, None, "chan"),
        P("chan"),
        P("date", "chan", None),
        P(),
        P(),
        P(("groups", "pix"), ("date", "chan")),
    )
    sizes = mesh.shape
    body = shards
    if sizes["pix"] == 2 and sizes["chan"] == 2 and sizes["date"] == 4:
        body = functools.partial(fused_shards, sizes["date"], sizes["chan"])
    return jax.shard_map(
        body,
        mesh=mesh,
        in_specs=placed,
        out_specs=(
            P(("groups", "pix"), ("date", "chan")),
            P("groups", None, None, "chan"),
            P("date", "chan", "groups"),
        ),
        check_vma=False,
    )
```

```python
import functools

import jax
import jax.numpy as jnp
from jax import lax
from jax.experimental import pallas as pl
from jax.experimental.pallas import tpu as pltpu
from jax.sharding import PartitionSpec as P

MESH = pl.DeviceIdType.MESH
CHUNK = 8


def fused(
    dates_n, chan_n, frames, sw, sb, tw, tb, hw, labels, logits_out, gs_out, gt_out,
    xpad, sw_v, sb_v, tw_v, tb_v, hw_v, lab_v, wbig, tw_m, hid, dact, gsh,
    lab_all, feat_all, gt_all, dwb, rs_all, ag_all,
    loc_sem, halo_send, halo_recv, fwd_send, fwd_recv, lab_send, lab_recv, feat_send, feat_recv,
    gt_send, gt_recv, rs_send, rs_recv, ag_send, ag_recv,
):
    f32, bf16 = jnp.float32, jnp.bfloat16
    dates, _, channels, cols = frames.shape
    outs = sw.shape[2]
    feats = tw.shape[1]
    half = dates // chan_n
    d, p, c = lax.axis_index("date"), lax.axis_index("pix"), lax.axis_index("chan")

    def target(od, op, oc):
        return {
            "date": lax.rem(d + od, dates_n),
            "pix": lax.rem(p + op, 2),
            "chan": lax.rem(c + oc, chan_n),
        }

    def remote(src, dst, send, recv, where):
        return pltpu.make_async_remote_copy(
            src_ref=src, dst_ref=dst, send_sem=send, recv_sem=recv, device_id=where, device_id_type=MESH
        )

    barrier = pltpu.get_barrier_semaphore()
    partners = [
        (od, op, oc)
        for od in range(dates_n)
        for op in range(2)
        for oc in range(chan_n)
        if (od or op or oc) and not (op and oc)
    ]
    for offs in partners:
        pl.semaphore_signal(barrier, inc=1, device_id=target(*offs), device_id_type=MESH)

    loads = [
        pltpu.make_async_copy(src, dst, loc_sem.at[i])
        for i, (src, dst) in enumerate(
            [
                (frames, xpad.at[:, pl.ds(1, 2)]),
                (sw, sw_v),
                (sb, sb_v),
                (tw, tw_v),
                (tb, tb_v),
                (hw, hw_v),
                (labels, lab_v),
            ]
        )
    ]
    for load in loads:
        load.start()
    pl.semaphore_wait(barrier, len(partners))

    halo, passed = [], []
    for k in range(half // CHUNK):
        mine = pl.ds(c * half + k * CHUNK, CHUNK)
        halo.append(
            remote(
                frames.at[mine, 1 - p], xpad.at[mine, 3 * p], halo_send.at[k], halo_recv.at[k], target(0, 1, 0)
            )
        )
        edge = xpad.at[mine, 3 - 3 * p]
        passed.append(remote(edge, edge, fwd_send.at[k], fwd_recv.at[k], target(0, 0, 1)))
        halo[k].start()

    block = d * chan_n + c
    width = lab_v.shape[1]
    blocks = dates_n * chan_n
    group = [(od, oc) for od in reversed(range(dates_n)) for oc in reversed(range(chan_n)) if od or oc]
    loads[6].wait()
    lane = lax.broadcasted_iota(jnp.int32, (2, cols), 1)
    inside = (lane >= block * width) & (lane < (block + 1) * width)
    spread = jnp.concatenate([lab_v[...].astype(f32)] * blocks, axis=1)
    lab_all[block] = jnp.concatenate([jnp.where(inside, spread, 0.0), jnp.zeros((6, cols), f32)], axis=0)
    lab_copies = [
        remote(lab_all.at[block], lab_all.at[block], lab_send.at[n], lab_recv.at[n], target(od, 0, oc))
        for n, (od, oc) in enumerate(group)
    ]
    for copy in lab_copies:
        copy.start()

    xpad[:, 3 * p] = jnp.zeros((dates, channels, cols), bf16)
    for n in range(1, 6):
        loads[n].wait()
    for a in range(3):
        for b in range(3):
            tap = sw_v[a, b].astype(f32)
            wbig[b * outs : (b + 1) * outs, a * channels : (a + 1) * channels] = tap
    conv = wbig[...].astype(bf16)
    def column(row, n):
        same = lax.broadcasted_iota(jnp.int32, (n, n), 0) == lax.broadcasted_iota(jnp.int32, (n, n), 1)
        return jnp.sum(jnp.where(same, row, 0.0), axis=1, keepdims=True)
    bias_o = column(sb_v[...], outs)
    bias_f = column(tb_v[...], feats)
    head = column(hw_v[...], feats)
    tw_f = jnp.concatenate([tw_v[t].astype(f32) for t in range(dates)], axis=1)
    tw_t = tw_f.astype(bf16)
    tw_m[...] = tw_f.T.astype(bf16)
    lane_o = lax.broadcasted_iota(jnp.int32, (outs, cols), 1)
    first, last = lane_o == 0, lane_o == cols - 1

    def right(x):
        return jnp.where(first, 0.0, pltpu.roll(x, 1, 1))

    def left(x):
        return jnp.where(last, 0.0, pltpu.roll(x, cols - 1, 1))

    def forward(start, row):
        x = xpad[pl.ds(start, CHUNK), pl.ds(row, 3)].reshape(CHUNK, 3 * channels, cols)
        z = jnp.dot(
            conv, jnp.concatenate([x[n] for n in range(CHUNK)], axis=1), preferred_element_type=f32
        )
        for n in range(CHUNK):
            tap = [z[b * outs : (b + 1) * outs, n * cols : (n + 1) * cols] for b in range(3)]
            pre = tap[1] + right(tap[0]) + left(tap[2]) + bias_o
            sig = jax.nn.sigmoid(pre)
            hid[row, start + n] = (pre * sig).astype(bf16)
            dact[row, start + n] = sig * (1.0 + pre * (1.0 - sig))

    def spread_partial(step, row):
        part = jnp.dot(tw_t, hid[row].reshape(dates * outs, cols), preferred_element_type=f32)
        feat_all[row, block] = part.astype(bf16)
        mine = feat_all.at[row, block]
        copies = [
            remote(mine, mine, feat_send.at[step, n], feat_recv.at[step, n], target(od, 0, oc))
            for n, (od, oc) in enumerate(group)
        ]
        for copy in copies:
            copy.start()
        return copies

    loads[0].wait()
    for t in range(0, dates, CHUNK):
        forward(t, p)
    feat_copies = spread_partial(0, p)

    other = 1 - c
    steps = half // CHUNK
    for k in range(steps):
        halo[k].wait_recv()
        passed[k].start()
        forward(c * half + k * CHUNK, 1 - p)
        if k:
            passed[k - 1].wait_recv()
            forward(other * half + (k - 1) * CHUNK, 1 - p)
    passed[steps - 1].wait_recv()
    forward(other * half + (steps - 1) * CHUNK, 1 - p)
    feat_copies += spread_partial(1, 1 - p)

    for copy in lab_copies:
        copy.wait_recv()
    lab = jnp.sum(lab_all[...], axis=0)
    for copy in feat_copies:
        copy.wait_recv()

    grads, rows_out = [], []
    for i in range(2):
        feature = jnp.sum(feat_all[i].astype(f32), axis=0) + bias_f
        sig = jax.nn.sigmoid(feature)
        logit = jnp.sum(feature * sig * head, axis=0, keepdims=True)
        dlogit = jax.nn.sigmoid(logit) - lab[i : i + 1]
        rows_out.append(logit)
        grads.append((dlogit * head * sig * (1.0 + feature * (1.0 - sig))).astype(bf16))
    fgrad = jnp.concatenate(grads, axis=1)

    contract = (((1,), (1,)), ((), ()))

    for t in range(0, dates, CHUNK):
        hgrad = jnp.dot(
            tw_m[t * outs : (t + CHUNK) * outs], fgrad, preferred_element_type=f32
        )
        for n in range(CHUNK):
            for i in range(2):
                g = hgrad[n * outs : (n + 1) * outs, i * cols : (i + 1) * cols] * dact[i, t + n]
                g = g.astype(bf16).astype(f32)
                at = slice((t + n) * cols, (t + n + 1) * cols)
                for b, v in enumerate((left(g), g, right(g))):
                    row = (i * 3 + b) * outs
                    gsh[row : row + outs, at] = v.astype(bf16)
    x_all = jnp.concatenate(
        [xpad[t].reshape(4 * channels, cols) for t in range(dates)], axis=1
    )
    dt = lax.dot_general(gsh[...], x_all, contract, preferred_element_type=f32)
    dw = dt[: 3 * outs] + pltpu.roll(dt[3 * outs :], 3 * channels, 1)
    for b in range(3):
        for h in range(2):
            dwb[2 * b + h] = dw[b * outs : (b + 1) * outs, h * 128 : (h + 1) * 128].astype(bf16)

    idx = d * 2 + p
    sums = dates_n * 2
    owners = dwb.shape[0]
    shift = (sums - owners) // 2
    mine = idx - shift
    is_owner = (mine >= 0) & (mine < owners)

    def rs_copy(k):
        to = {"date": (k + shift) // 2, "pix": (k + shift) % 2, "chan": c}
        return remote(
            dwb.at[k], rs_all.at[idx], rs_send.at[k], rs_recv.at[idx], to
        )

    for k in range(owners):
        @pl.when(mine != k)
        def _():
            rs_copy(k).start()

    gt_all[p] = lax.dot_general(
        fgrad, jnp.concatenate([hid[i].reshape(dates * outs, cols) for i in range(2)], axis=1), contract, preferred_element_type=f32
    )
    gt_copy = remote(gt_all.at[p], gt_all.at[p], gt_send, gt_recv, target(0, 1, 0))
    gt_copy.start()

    all_other = [(od, op) for od in reversed(range(dates_n)) for op in reversed(range(2)) if od or op]

    def ag_copies():
        return [
            remote(ag_all.at[mine], ag_all.at[mine], ag_send.at[n], ag_recv.at[mine], target(od, op, 0))
            for n, (od, op) in enumerate(all_other)
        ]

    @pl.when(is_owner)
    def _():
        rs_all[idx] = dwb[mine]
        for q in range(sums):
            @pl.when(idx != q)
            def _():
                pltpu.make_async_copy(rs_all.at[q], rs_all.at[q], rs_recv.at[q]).wait()
        ag_all[mine] = jnp.sum(rs_all[...].astype(f32), axis=0).astype(bf16)
        for copy in ag_copies():
            copy.start()

    gt_copy.wait_recv()
    gt_out[...] = gt_all[0] + gt_all[1]
    logit_rows = jnp.concatenate(rows_out + [jnp.zeros((6, cols), f32)], axis=0)
    moved = pltpu.roll(logit_rows, lax.rem(cols - block * width, cols), 1)
    logits_out[...] = moved[:2, :width]
    for copy in halo + passed + lab_copies + feat_copies + [gt_copy]:
        copy.wait_send()
    for k in range(owners):
        @pl.when(mine != k)
        def _():
            rs_copy(k).wait_send()

    for k in range(owners):
        @pl.when(mine != k)
        def _():
            pltpu.make_async_copy(ag_all.at[k], ag_all.at[k], ag_recv.at[k]).wait()
        gs_out[k] = ag_all[k]

    @pl.when(is_owner)
    def _():
        for copy in ag_copies():
            copy.wait_send()


def unpack(logits, gs, gt, logits_out, gs_out, gt_out):
    channels = gs_out.shape[3]
    outs = gt_out.shape[2]
    logits_out[...] = logits[...]
    for k in range(gs.shape[0]):
        piece = gs[k].astype(jnp.float32)
        for n in range(2 - k % 2):
            gs_out[2 * (k % 2) + n, k // 2] = piece[:, n * channels : (n + 1) * channels]
    for t in range(gt_out.shape[0]):
        gt_out[t] = gt[:, t * outs : (t + 1) * outs]


def fused_shards(dates_n, chan_n, frames, sw, sb, tw, tb, hw, labels):
    dates, rows, channels, cols = frames.shape
    outs, feats = sw.shape[3], tw.shape[2]
    sw, tw = sw.transpose(0, 1, 3, 2), tw.transpose(0, 2, 1)
    f32, bf16 = jnp.float32, jnp.bfloat16
    steps = dates // chan_n // CHUNK
    blocks, sums = dates_n * chan_n, dates_n * 2
    owners = 6
    dma = pltpu.SemaphoreType.DMA
    made = pl.pallas_call(
        functools.partial(fused, dates_n, chan_n),
        out_shape=(
            jax.ShapeDtypeStruct(labels.shape, f32),
            jax.ShapeDtypeStruct((owners, outs, 128), bf16),
            jax.ShapeDtypeStruct((feats, dates * outs), f32),
        ),
        in_specs=[pl.BlockSpec(memory_space=pltpu.HBM)] * 7,
        out_specs=[pl.BlockSpec(memory_space=pltpu.VMEM)] * 3,
        scratch_shapes=[
            pltpu.VMEM((dates, 4, channels, cols), bf16),
            pltpu.VMEM(sw.shape, bf16),
            pltpu.VMEM((1, outs), f32),
            pltpu.VMEM(tw.shape, bf16),
            pltpu.VMEM((1, feats), f32),
            pltpu.VMEM((1, feats), f32),
            pltpu.VMEM(labels.shape, jnp.int32),
            pltpu.VMEM((3 * outs, 3 * channels), f32),
            pltpu.VMEM((dates * outs, feats), bf16),
            pltpu.VMEM((2, dates, outs, cols), bf16),
            pltpu.VMEM((2, dates, outs, cols), f32),
            pltpu.VMEM((6 * outs, dates * cols), bf16),
            pltpu.VMEM((blocks, 8, cols), f32),
            pltpu.VMEM((2, blocks, feats, cols), bf16),
            pltpu.VMEM((2, feats, dates * outs), f32),
            pltpu.VMEM((owners, outs, 128), bf16),
            pltpu.VMEM((sums, outs, 128), bf16),
            pltpu.VMEM((owners, outs, 128), bf16),
            dma((7,)),
            dma((steps,)),
            dma((steps,)),
            dma((steps,)),
            dma((steps,)),
            dma((blocks,)),
            dma((blocks,)),
            dma((2, blocks)),
            dma((2, blocks)),
            dma,
            dma,
            dma((owners,)),
            dma((sums,)),
            dma((sums,)),
            dma((owners,)),
        ],
        compiler_params=pltpu.CompilerParams(
            collective_id=0, has_side_effects=True, vmem_limit_bytes=56_400_000
        ),
    )(frames, sw, sb[None], tw, tb[None], hw[None], labels)
    logits, gs, gt = pl.pallas_call(
        unpack,
        out_shape=tuple(jax.ShapeDtypeStruct(shape, f32) for shape in (labels.shape, sw.shape, tw.shape)),
        in_specs=[pl.BlockSpec(memory_space=pltpu.VMEM)] * 3,
        out_specs=[pl.BlockSpec(memory_space=pltpu.VMEM)] * 3,
        compiler_params=pltpu.CompilerParams(vmem_limit_bytes=1 << 20),
    )(*made)
    return logits, gs.transpose(0, 1, 3, 2), gt.transpose(0, 2, 1)


def with_halo(block, sides, width):
    for axis, dim in sides:
        count = lax.axis_size(axis)
        forward = [(i, i + 1) for i in range(count - 1)]
        backward = [(target, source) for source, target in forward]
        low = lax.ppermute(
            lax.slice_in_dim(block, block.shape[dim] - width, None, axis=dim), axis, forward
        )
        high = lax.ppermute(lax.slice_in_dim(block, 0, width, axis=dim), axis, backward)
        block = jnp.concatenate([low, block, high], axis=dim)
    return block


def shards(
    frames, spatial_weight, spatial_bias, temporal_weight, temporal_bias, head_weight, labels
):
    dates_here, rows, channels, columns = frames.shape
    padded = with_halo(frames, (("pix", 1),), 1)
    padded = jnp.pad(padded, ((0, 0), (0, 0), (0, 0), (1, 1)))
    preact = spatial_bias[None, None, :, None]
    for row_off in range(3):
        for col_off in range(3):
            window = padded[:, row_off : row_off + rows, :, col_off : col_off + columns]
            preact = preact + jnp.einsum(
                "ticj,co->tioj",
                window,
                spatial_weight[row_off, col_off],
                preferred_element_type=jnp.float32,
            )
    sigmoid_pre = jax.nn.sigmoid(preact)
    hidden = (preact * sigmoid_pre).astype(jnp.bfloat16)
    partial_feat = jnp.einsum(
        "tioj,tof->fij", hidden, temporal_weight, preferred_element_type=jnp.float32
    )
    feature = (
        lax.psum_scatter(partial_feat, ("date", "chan"), scatter_dimension=2, tiled=True)
        + temporal_bias[:, None, None]
    )
    sigmoid_feat = jax.nn.sigmoid(feature)
    logits = jnp.einsum("fij,f->ij", feature * sigmoid_feat, head_weight)
    dlogit = jax.nn.sigmoid(logits) - labels.astype(jnp.float32)
    feature_grad = (
        dlogit[None]
        * head_weight[:, None, None]
        * sigmoid_feat
        * (1.0 + feature * (1.0 - sigmoid_feat))
    ).astype(jnp.bfloat16)
    full_grad = lax.all_gather(feature_grad, ("date", "chan"), axis=2, tiled=True)
    temporal_part = jnp.einsum(
        "tioj,fij->tof", hidden, full_grad, preferred_element_type=jnp.float32
    )
    hidden_grad = jnp.einsum(
        "fij,tof->tioj", full_grad, temporal_weight, preferred_element_type=jnp.float32
    )
    preact_grad = (hidden_grad * sigmoid_pre * (1.0 + preact * (1.0 - sigmoid_pre))).astype(
        jnp.bfloat16
    )
    rows_out = []
    for row_off in range(3):
        cols_out = []
        for col_off in range(3):
            window = padded[:, row_off : row_off + rows, :, col_off : col_off + columns]
            cols_out.append(
                jnp.einsum("ticj,tioj->co", window, preact_grad, preferred_element_type=jnp.float32)
            )
        rows_out.append(jnp.stack(cols_out))
    spatial_part = jnp.stack(rows_out)
    grad_temporal = lax.psum(temporal_part, "pix")
    grad_spatial = lax.psum(spatial_part, ("date", "pix"))
    return (logits, grad_spatial, grad_temporal)


def solution(mesh):
    placed = (
        P(("groups", "date"), "pix", None, None),
        P(None, None, None, "chan"),
        P("chan"),
        P("date", "chan", None),
        P(),
        P(),
        P(("groups", "pix"), ("date", "chan")),
    )
    sizes = mesh.shape
    body = shards
    if sizes["pix"] == 2 and sizes["chan"] == 2 and sizes["date"] == 4:
        body = functools.partial(fused_shards, sizes["date"], sizes["chan"])
    return jax.shard_map(
        body,
        mesh=mesh,
        in_specs=placed,
        out_specs=(
            P(("groups", "pix"), ("date", "chan")),
            P("groups", None, None, "chan"),
            P("date", "chan", "groups"),
        ),
        check_vma=False,
    )
```

```python
import functools

import jax
import jax.numpy as jnp
from jax import lax
from jax.experimental import pallas as pl
from jax.experimental.pallas import tpu as pltpu
from jax.sharding import PartitionSpec as P

MESH = pl.DeviceIdType.MESH
CHUNK = 8


def fused(
    dates_n, chan_n, frames, sw, sb, tw, tb, hw, labels, logits_out, gs_out, gt_out,
    xpad, sw_v, sb_v, tw_v, tb_v, hw_v, lab_v, wbig, tw_m, hid, dact, gsh,
    lab_all, feat_all, gt_all, dwb, rs_all, ag_all,
    loc_sem, halo_send, halo_recv, fwd_send, fwd_recv, lab_send, lab_recv, feat_send, feat_recv,
    gt_send, gt_recv, rs_send, rs_recv, ag_send, ag_recv,
):
    f32, bf16 = jnp.float32, jnp.bfloat16
    dates, _, channels, cols = frames.shape
    outs = sw.shape[2]
    feats = tw.shape[1]
    half = dates // chan_n
    d, p, c = lax.axis_index("date"), lax.axis_index("pix"), lax.axis_index("chan")

    def target(od, op, oc):
        return {
            "date": lax.rem(d + od, dates_n),
            "pix": lax.rem(p + op, 2),
            "chan": lax.rem(c + oc, chan_n),
        }

    def remote(src, dst, send, recv, where):
        return pltpu.make_async_remote_copy(
            src_ref=src, dst_ref=dst, send_sem=send, recv_sem=recv, device_id=where, device_id_type=MESH
        )

    barrier = pltpu.get_barrier_semaphore()
    partners = [
        (od, op, oc)
        for od in range(dates_n)
        for oc in range(chan_n)
        for op in range(2)
        if (od or op or oc) and not (op and oc)
    ]
    for offs in partners:
        pl.semaphore_signal(barrier, inc=1, device_id=target(*offs), device_id_type=MESH)

    loads = [
        pltpu.make_async_copy(src, dst, loc_sem.at[i])
        for i, (src, dst) in enumerate(
            [
                (frames, xpad.at[:, pl.ds(1, 2)]),
                (sw, sw_v),
                (sb, sb_v),
                (tw, tw_v),
                (tb, tb_v),
                (hw, hw_v),
                (labels, lab_v),
            ]
        )
    ]
    for load in loads:
        load.start()
    pl.semaphore_wait(barrier, len(partners))

    halo, passed = [], []
    for k in range(half // CHUNK):
        mine = pl.ds(c * half + k * CHUNK, CHUNK)
        halo.append(
            remote(
                frames.at[mine, 1 - p], xpad.at[mine, 3 * p], halo_send.at[k], halo_recv.at[k], target(0, 1, 0)
            )
        )
        edge = xpad.at[mine, 3 - 3 * p]
        passed.append(remote(edge, edge, fwd_send.at[k], fwd_recv.at[k], target(0, 0, 1)))
        halo[k].start()

    block = d * chan_n + c
    width = lab_v.shape[1]
    blocks = dates_n * chan_n
    group = [(od, oc) for od in reversed(range(dates_n)) for oc in reversed(range(chan_n)) if od or oc]
    loads[6].wait()
    lane = lax.broadcasted_iota(jnp.int32, (2, cols), 1)
    inside = (lane >= block * width) & (lane < (block + 1) * width)
    spread = jnp.concatenate([lab_v[...].astype(f32)] * blocks, axis=1)
    lab_all[block] = jnp.concatenate([jnp.where(inside, spread, 0.0), jnp.zeros((6, cols), f32)], axis=0)
    lab_copies = [
        remote(lab_all.at[block], lab_all.at[block], lab_send.at[n], lab_recv.at[n], target(od, 0, oc))
        for n, (od, oc) in enumerate(group)
    ]
    for copy in lab_copies:
        copy.start()

    xpad[:, 3 * p] = jnp.zeros((dates, channels, cols), bf16)
    for n in range(1, 6):
        loads[n].wait()
    for a in range(3):
        for b in range(3):
            tap = sw_v[a, b].astype(f32)
            wbig[b * outs : (b + 1) * outs, a * channels : (a + 1) * channels] = tap
    conv = wbig[...].astype(bf16)
    def column(row, n):
        same = lax.broadcasted_iota(jnp.int32, (n, n), 0) == lax.broadcasted_iota(jnp.int32, (n, n), 1)
        return jnp.sum(jnp.where(same, row, 0.0), axis=1, keepdims=True)
    bias_o = column(sb_v[...], outs)
    bias_f = column(tb_v[...], feats)
    head = column(hw_v[...], feats)
    tw_f = jnp.concatenate([tw_v[t].astype(f32) for t in range(dates)], axis=1)
    tw_t = tw_f.astype(bf16)
    tw_m[...] = tw_f.T.astype(bf16)
    lane_o = lax.broadcasted_iota(jnp.int32, (outs, cols), 1)
    first, last = lane_o == 0, lane_o == cols - 1

    def right(x):
        return jnp.where(first, 0.0, pltpu.roll(x, 1, 1))

    def left(x):
        return jnp.where(last, 0.0, pltpu.roll(x, cols - 1, 1))

    def forward(start, row):
        x = xpad[pl.ds(start, CHUNK), pl.ds(row, 3)].reshape(CHUNK, 3 * channels, cols)
        z = jnp.dot(
            conv, jnp.concatenate([x[n] for n in range(CHUNK)], axis=1), preferred_element_type=f32
        )
        for n in range(CHUNK):
            tap = [z[b * outs : (b + 1) * outs, n * cols : (n + 1) * cols] for b in range(3)]
            pre = tap[1] + right(tap[0]) + left(tap[2]) + bias_o
            sig = jax.nn.sigmoid(pre)
            hid[row, start + n] = (pre * sig).astype(bf16)
            dact[row, start + n] = sig * (1.0 + pre * (1.0 - sig))

    def spread_partial(step, row):
        part = jnp.dot(tw_t, hid[row].reshape(dates * outs, cols), preferred_element_type=f32)
        feat_all[row, block] = part.astype(bf16)
        mine = feat_all.at[row, block]
        copies = [
            remote(mine, mine, feat_send.at[step, n], feat_recv.at[step, n], target(od, 0, oc))
            for n, (od, oc) in enumerate(group)
        ]
        for copy in copies:
            copy.start()
        return copies

    loads[0].wait()
    for t in range(0, dates, CHUNK):
        forward(t, p)
    feat_copies = spread_partial(0, p)

    other = 1 - c
    steps = half // CHUNK
    for k in range(steps):
        halo[k].wait_recv()
        passed[k].start()
        forward(c * half + k * CHUNK, 1 - p)
        if k:
            passed[k - 1].wait_recv()
            forward(other * half + (k - 1) * CHUNK, 1 - p)
    passed[steps - 1].wait_recv()
    forward(other * half + (steps - 1) * CHUNK, 1 - p)
    feat_copies += spread_partial(1, 1 - p)

    for copy in lab_copies:
        copy.wait_recv()
    lab = jnp.sum(lab_all[...], axis=0)
    for copy in feat_copies:
        copy.wait_recv()

    grads, rows_out = [], []
    for i in range(2):
        feature = jnp.sum(feat_all[i].astype(f32), axis=0) + bias_f
        sig = jax.nn.sigmoid(feature)
        logit = jnp.sum(feature * sig * head, axis=0, keepdims=True)
        dlogit = jax.nn.sigmoid(logit) - lab[i : i + 1]
        rows_out.append(logit)
        grads.append((dlogit * head * sig * (1.0 + feature * (1.0 - sig))).astype(bf16))
    fgrad = jnp.concatenate(grads, axis=1)

    contract = (((1,), (1,)), ((), ()))

    for t in range(0, dates, CHUNK):
        hgrad = jnp.dot(
            tw_m[t * outs : (t + CHUNK) * outs], fgrad, preferred_element_type=f32
        )
        for n in range(CHUNK):
            for i in range(2):
                g = hgrad[n * outs : (n + 1) * outs, i * cols : (i + 1) * cols] * dact[i, t + n]
                g = g.astype(bf16).astype(f32)
                at = slice((t + n) * cols, (t + n + 1) * cols)
                for b, v in enumerate((left(g), g, right(g))):
                    row = (i * 3 + b) * outs
                    gsh[row : row + outs, at] = v.astype(bf16)
    x_all = jnp.concatenate(
        [xpad[t].reshape(4 * channels, cols) for t in range(dates)], axis=1
    )
    dt = lax.dot_general(gsh[...], x_all, contract, preferred_element_type=f32)
    dw = dt[: 3 * outs] + pltpu.roll(dt[3 * outs :], 3 * channels, 1)
    for b in range(3):
        dwb[b] = dw[b * outs : (b + 1) * outs, :128].astype(bf16)
    rest = [dw[b * outs : (b + 1) * outs, 128:192] for b in range(3)]
    dwb[3] = jnp.concatenate(rest[:2], axis=1).astype(bf16)
    dwb[4] = jnp.concatenate([rest[2], jnp.zeros_like(rest[2])], axis=1).astype(bf16)

    idx = d * 2 + p
    sums = dates_n * 2
    owners = dwb.shape[0]
    shift = (sums - owners) // 2
    mine = idx - shift
    is_owner = (mine >= 0) & (mine < owners)

    def rs_copy(k):
        to = {"date": (k + shift) // 2, "pix": (k + shift) % 2, "chan": c}
        return remote(
            dwb.at[k], rs_all.at[idx], rs_send.at[k], rs_recv.at[idx], to
        )

    for k in range(owners):
        @pl.when(mine != k)
        def _():
            rs_copy(k).start()

    gt_all[p] = lax.dot_general(
        fgrad, jnp.concatenate([hid[i].reshape(dates * outs, cols) for i in range(2)], axis=1), contract, preferred_element_type=f32
    )
    gt_copy = remote(gt_all.at[p], gt_all.at[p], gt_send, gt_recv, target(0, 1, 0))
    gt_copy.start()

    all_other = [(od, op) for od in reversed(range(dates_n)) for op in reversed(range(2)) if od or op]

    def ag_copies():
        return [
            remote(ag_all.at[mine], ag_all.at[mine], ag_send.at[n], ag_recv.at[mine], target(od, op, 0))
            for n, (od, op) in enumerate(all_other)
        ]

    @pl.when(is_owner)
    def _():
        rs_all[idx] = dwb[mine]
        for q in range(sums):
            @pl.when(idx != q)
            def _():
                pltpu.make_async_copy(rs_all.at[q], rs_all.at[q], rs_recv.at[q]).wait()
        ag_all[mine] = jnp.sum(rs_all[...].astype(f32), axis=0).astype(bf16)
        for copy in ag_copies():
            copy.start()

    gt_copy.wait_recv()
    gt_out[...] = gt_all[0] + gt_all[1]
    logit_rows = jnp.concatenate(rows_out + [jnp.zeros((6, cols), f32)], axis=0)
    moved = pltpu.roll(logit_rows, lax.rem(cols - block * width, cols), 1)
    logits_out[...] = moved[:2, :width]
    for copy in halo + passed + lab_copies + feat_copies + [gt_copy]:
        copy.wait_send()
    for k in range(owners):
        @pl.when(mine != k)
        def _():
            rs_copy(k).wait_send()

    for k in range(owners):
        @pl.when(mine != k)
        def _():
            pltpu.make_async_copy(ag_all.at[k], ag_all.at[k], ag_recv.at[k]).wait()
        gs_out[k] = ag_all[k]

    @pl.when(is_owner)
    def _():
        for copy in ag_copies():
            copy.wait_send()


def unpack(logits, gs, gt, logits_out, gs_out, gt_out):
    channels = gs_out.shape[3]
    outs = gt_out.shape[2]
    logits_out[...] = logits[...]
    for k in range(gs.shape[0]):
        piece = gs[k].astype(jnp.float32)
        for n in range(2 if k < 4 else 1):
            a, b = (n, k) if k < 3 else (2, 2 * (k - 3) + n)
            gs_out[a, b] = piece[:, n * channels : (n + 1) * channels]
    for t in range(gt_out.shape[0]):
        gt_out[t] = gt[:, t * outs : (t + 1) * outs]


def fused_shards(dates_n, chan_n, frames, sw, sb, tw, tb, hw, labels):
    dates, rows, channels, cols = frames.shape
    outs, feats = sw.shape[3], tw.shape[2]
    sw, tw = sw.transpose(0, 1, 3, 2), tw.transpose(0, 2, 1)
    f32, bf16 = jnp.float32, jnp.bfloat16
    steps = dates // chan_n // CHUNK
    blocks, sums = dates_n * chan_n, dates_n * 2
    owners = 5
    dma = pltpu.SemaphoreType.DMA
    made = pl.pallas_call(
        functools.partial(fused, dates_n, chan_n),
        out_shape=(
            jax.ShapeDtypeStruct(labels.shape, f32),
            jax.ShapeDtypeStruct((owners, outs, 128), bf16),
            jax.ShapeDtypeStruct((feats, dates * outs), f32),
        ),
        in_specs=[pl.BlockSpec(memory_space=pltpu.HBM)] * 7,
        out_specs=[pl.BlockSpec(memory_space=pltpu.VMEM)] * 3,
        scratch_shapes=[
            pltpu.VMEM((dates, 4, channels, cols), bf16),
            pltpu.VMEM(sw.shape, bf16),
            pltpu.VMEM((1, outs), f32),
            pltpu.VMEM(tw.shape, bf16),
            pltpu.VMEM((1, feats), f32),
            pltpu.VMEM((1, feats), f32),
            pltpu.VMEM(labels.shape, jnp.int32),
            pltpu.VMEM((3 * outs, 3 * channels), f32),
            pltpu.VMEM((dates * outs, feats), bf16),
            pltpu.VMEM((2, dates, outs, cols), bf16),
            pltpu.VMEM((2, dates, outs, cols), f32),
            pltpu.VMEM((6 * outs, dates * cols), bf16),
            pltpu.VMEM((blocks, 8, cols), f32),
            pltpu.VMEM((2, blocks, feats, cols), bf16),
            pltpu.VMEM((2, feats, dates * outs), f32),
            pltpu.VMEM((owners, outs, 128), bf16),
            pltpu.VMEM((sums, outs, 128), bf16),
            pltpu.VMEM((owners, outs, 128), bf16),
            dma((7,)),
            dma((steps,)),
            dma((steps,)),
            dma((steps,)),
            dma((steps,)),
            dma((blocks,)),
            dma((blocks,)),
            dma((2, blocks)),
            dma((2, blocks)),
            dma,
            dma,
            dma((owners,)),
            dma((sums,)),
            dma((sums,)),
            dma((owners,)),
        ],
        compiler_params=pltpu.CompilerParams(
            collective_id=0, has_side_effects=True, vmem_limit_bytes=56_400_000
        ),
    )(frames, sw, sb[None], tw, tb[None], hw[None], labels)
    logits, gs, gt = pl.pallas_call(
        unpack,
        out_shape=tuple(jax.ShapeDtypeStruct(shape, f32) for shape in (labels.shape, sw.shape, tw.shape)),
        in_specs=[pl.BlockSpec(memory_space=pltpu.VMEM)] * 3,
        out_specs=[pl.BlockSpec(memory_space=pltpu.VMEM)] * 3,
        compiler_params=pltpu.CompilerParams(vmem_limit_bytes=1 << 20),
    )(*made)
    return logits, gs.transpose(0, 1, 3, 2), gt.transpose(0, 2, 1)


def with_halo(block, sides, width):
    for axis, dim in sides:
        count = lax.axis_size(axis)
        forward = [(i, i + 1) for i in range(count - 1)]
        backward = [(target, source) for source, target in forward]
        low = lax.ppermute(
            lax.slice_in_dim(block, block.shape[dim] - width, None, axis=dim), axis, forward
        )
        high = lax.ppermute(lax.slice_in_dim(block, 0, width, axis=dim), axis, backward)
        block = jnp.concatenate([low, block, high], axis=dim)
    return block


def shards(
    frames, spatial_weight, spatial_bias, temporal_weight, temporal_bias, head_weight, labels
):
    dates_here, rows, channels, columns = frames.shape
    padded = with_halo(frames, (("pix", 1),), 1)
    padded = jnp.pad(padded, ((0, 0), (0, 0), (0, 0), (1, 1)))
    preact = spatial_bias[None, None, :, None]
    for row_off in range(3):
        for col_off in range(3):
            window = padded[:, row_off : row_off + rows, :, col_off : col_off + columns]
            preact = preact + jnp.einsum(
                "ticj,co->tioj",
                window,
                spatial_weight[row_off, col_off],
                preferred_element_type=jnp.float32,
            )
    sigmoid_pre = jax.nn.sigmoid(preact)
    hidden = (preact * sigmoid_pre).astype(jnp.bfloat16)
    partial_feat = jnp.einsum(
        "tioj,tof->fij", hidden, temporal_weight, preferred_element_type=jnp.float32
    )
    feature = (
        lax.psum_scatter(partial_feat, ("date", "chan"), scatter_dimension=2, tiled=True)
        + temporal_bias[:, None, None]
    )
    sigmoid_feat = jax.nn.sigmoid(feature)
    logits = jnp.einsum("fij,f->ij", feature * sigmoid_feat, head_weight)
    dlogit = jax.nn.sigmoid(logits) - labels.astype(jnp.float32)
    feature_grad = (
        dlogit[None]
        * head_weight[:, None, None]
        * sigmoid_feat
        * (1.0 + feature * (1.0 - sigmoid_feat))
    ).astype(jnp.bfloat16)
    full_grad = lax.all_gather(feature_grad, ("date", "chan"), axis=2, tiled=True)
    temporal_part = jnp.einsum(
        "tioj,fij->tof", hidden, full_grad, preferred_element_type=jnp.float32
    )
    hidden_grad = jnp.einsum(
        "fij,tof->tioj", full_grad, temporal_weight, preferred_element_type=jnp.float32
    )
    preact_grad = (hidden_grad * sigmoid_pre * (1.0 + preact * (1.0 - sigmoid_pre))).astype(
        jnp.bfloat16
    )
    rows_out = []
    for row_off in range(3):
        cols_out = []
        for col_off in range(3):
            window = padded[:, row_off : row_off + rows, :, col_off : col_off + columns]
            cols_out.append(
                jnp.einsum("ticj,tioj->co", window, preact_grad, preferred_element_type=jnp.float32)
            )
        rows_out.append(jnp.stack(cols_out))
    spatial_part = jnp.stack(rows_out)
    grad_temporal = lax.psum(temporal_part, "pix")
    grad_spatial = lax.psum(spatial_part, ("date", "pix"))
    return (logits, grad_spatial, grad_temporal)


def solution(mesh):
    placed = (
        P(("groups", "date"), "pix", None, None),
        P(None, None, None, "chan"),
        P("chan"),
        P("date", "chan", None),
        P(),
        P(),
        P(("groups", "pix"), ("date", "chan")),
    )
    sizes = mesh.shape
    body = shards
    if sizes["pix"] == 2 and sizes["chan"] == 2 and sizes["date"] == 4:
        body = functools.partial(fused_shards, sizes["date"], sizes["chan"])
    return jax.shard_map(
        body,
        mesh=mesh,
        in_specs=placed,
        out_specs=(
            P(("groups", "pix"), ("date", "chan")),
            P("groups", None, None, "chan"),
            P("date", "chan", "groups"),
        ),
        check_vma=False,
    )
```
